256 devices in a mesh: section: 16 (over x_hi, y, core), dp: 16 (over z, x_lo).
Axes of the slice: x: 4 (x_hi: 2, x_lo: 2; x = x_hi * 2 + x_lo), y: 4, z: 8, core: 2. Of those that a mesh axis runs over, the one named last changes fastest.
Arguments:
- entering: bfloat16 [2, 4, 256, 8192], P(None, None, 'dp'), may hold values from -6 to 6
- cotangent: bfloat16 [2, 4, 256, 8192], P(None, None, 'dp'), may hold values from -6 to 6
- down_proj: bfloat16 [16, 8192, 256], P('section', 'dp'), may hold values from -0.0625 to 0.0625
- up_proj: bfloat16 [16, 256, 8192], P('section', None, 'dp'), may hold values from -0.375 to 0.375
Outputs:
- grad_down: float32 [16, 8192, 256], P('section', 'dp')
- grad_up: float32 [16, 256, 8192], P('section', None, 'dp')
The draws below stay inside these ranges and needn't reach their ends.
All inputs are finite; a program needn't handle non-finite values.
Results may differ from the reference program's by a relative error of at most 0.035.
Values may be sent and summed in bfloat16 or wider, within the bound.
No kernel may reach another device: no remote copies, remote signals or barrier semaphores. Data moves between devices by JAX's collectives and lax.ppermute only.
A program may use at most 128 MiB of HBM per device.

```python
import jax
import jax.numpy as jnp
from jax import lax

D = 8192
R = 256
MB = 4
ROWS = 16
TOKENS = 256
N_SECTION = 16
N_DP = 16


def shard_levels(own_key, dims, split, low, high):
    loudness, own = 1.0, jax.random.fold_in(own_key, 6)
    for position, blocks in split:
        draws = jnp.exp(jax.random.uniform(jax.random.fold_in(own, position), (blocks,), jnp.float32, low / len(split), high / len(split)))
        loudness = loudness * jnp.repeat(draws, dims[position] // blocks).reshape([-1 if axis == position else 1 for axis in range(len(dims))])
    return loudness


def noise(stream_key, shape, deviation, bound, cuts=(), held_as=jnp.bfloat16):
    array = jax.random.normal(stream_key, shape, jnp.float32) * deviation
    if len(cuts) > 0:
        array = shard_levels(stream_key, shape, cuts, -0.22, 0.18) * array
    return jnp.clip(array, min=-bound, max=bound).astype(held_as)


def setup_inputs(seed: int = 0) -> dict:
    arg_keys = jax.random.split(jax.random.key(seed), 5)
    entering = noise(arg_keys[0], (2, MB, TOKENS, D), 1.0, 6.0, ((2, 16),))
    cotangent = noise(arg_keys[1], (2, MB, TOKENS, D), 1.0, 6.0, ((2, 16),))
    down_proj = noise(arg_keys[2], (N_SECTION, D, R), D ** -0.5, 0.0625, ((0, 16), (1, 16)))
    up_proj = noise(arg_keys[3], (N_SECTION, R, D), R ** -0.5, 0.375, ((0, 16), (2, 16)))
    return dict(entering=entering, cotangent=cotangent, down_proj=down_proj, up_proj=up_proj)


epsilon = 1e-05
root_half = 0.7071067811865476
inv_root_tau = 0.3989422804014327

def gelu_value(values):
    return 0.5 * values * (1.0 + lax.erf(values * root_half))

def gelu_slope(values):
    return 0.5 * (1.0 + lax.erf(values * root_half)) + values * inv_root_tau * jnp.exp(-0.5 * values * values)

def layer_forward(hidden, down_weight, up_weight):
    widened = hidden.astype(jnp.float32)
    scaling = lax.rsqrt(lax.optimization_barrier(jnp.mean(widened * widened, axis=-1, keepdims=True)) + epsilon)
    normed = (widened * scaling).astype(jnp.bfloat16)
    latent = jnp.dot(normed, down_weight, preferred_element_type=jnp.float32)
    active = gelu_value(latent).astype(jnp.bfloat16)
    return (widened + jnp.dot(active, up_weight, preferred_element_type=jnp.float32)).astype(jnp.bfloat16)

def layer_backward(hidden, incoming, down_weight, up_weight):
    widened = hidden.astype(jnp.float32)
    scaling = lax.rsqrt(lax.optimization_barrier(jnp.mean(widened * widened, axis=-1, keepdims=True)) + epsilon)
    unit_rows = widened * scaling
    normed = unit_rows.astype(jnp.bfloat16)
    latent = jnp.dot(normed, down_weight, preferred_element_type=jnp.float32)
    active = gelu_value(latent).astype(jnp.bfloat16)
    dactive = jnp.dot(incoming, up_weight.T, preferred_element_type=jnp.float32)
    dlatent = (dactive * gelu_slope(latent)).astype(jnp.bfloat16)
    unit_grad = jnp.dot(dlatent, down_weight.T, preferred_element_type=jnp.float32)
    inner = lax.optimization_barrier(jnp.mean(unit_grad * unit_rows, axis=-1, keepdims=True))
    passed = (incoming.astype(jnp.float32) + scaling * (unit_grad - unit_rows * inner)).astype(jnp.bfloat16)
    return (normed, dlatent, active, passed)

def reference(entering, cotangent, down_proj, up_proj):
    grad_down = jnp.zeros((N_SECTION, D, R), jnp.float32)
    grad_up = jnp.zeros((N_SECTION, R, D), jnp.float32)
    for direction in range(2):
        inputs = entering[direction].reshape(MB, N_DP, ROWS, D).transpose(1, 0, 2, 3).reshape(N_DP * MB * ROWS, D)
        seeds = cotangent[direction].reshape(MB, N_DP, ROWS, D).transpose(1, 0, 2, 3).reshape(N_DP * MB * ROWS, D)

        def forward_section(hidden, weights):
            return (layer_forward(hidden, weights[0], weights[1]), hidden)
        _, stored = lax.scan(forward_section, inputs, (down_proj, up_proj))

        def backward_section(incoming, pieces):
            down_weight, up_weight, hidden = pieces
            normed, dlatent, active, passed = layer_backward(hidden, incoming, down_weight, up_weight)
            per_down = jnp.einsum('rnd,rnk->rdk', normed.reshape(N_DP, MB * ROWS, D).astype(jnp.float32), dlatent.reshape(N_DP, MB * ROWS, R).astype(jnp.float32))
            per_up = jnp.einsum('rnk,rnd->rkd', active.reshape(N_DP, MB * ROWS, R).astype(jnp.float32), incoming.reshape(N_DP, MB * ROWS, D).astype(jnp.float32))
            per_down = lax.optimization_barrier(per_down.astype(jnp.bfloat16)).astype(jnp.float32).sum(0)
            per_up = lax.optimization_barrier(per_up.astype(jnp.bfloat16)).astype(jnp.float32).sum(0)
            return (passed, (per_down, per_up))
        _, (section_down, section_up) = lax.scan(backward_section, seeds, (down_proj, up_proj, stored), reverse=True)
        grad_down = grad_down + section_down
        grad_up = grad_up + section_up
    return (grad_down, grad_up)
```

```python
import functools

import jax
import jax.numpy as jnp
from jax import lax
from jax.experimental import pallas as pl
from jax.experimental.pallas import tpu as pltpu
from jax.sharding import PartitionSpec as P

epsilon = 1e-05
root_half = 0.7071067811865476
inv_root_tau = 0.3989422804014327

BF = jnp.bfloat16
F32 = jnp.float32
BOTH = ("section", "dp")
WIDTH = 8192
RANK = 256
BLOCK = 512
BLOCKS = WIDTH // BLOCK
ROWS = 32
LAYERS = 4
EXTRA = WIDTH + RANK
VMEM_LIMIT = 50 * 2**20

GROUPS = ((0,), (1, -1), (2, -2), (3, -3), (4,))
SINGLES = (0, 1, -1, 2, -2, 3, -3, 4)


def unpack(section, dp):
    return section // 8, (section // 2) % 4, section % 2, dp // 2, dp % 2


def pack(x_hi, y, core, z, x_lo):
    return (x_hi * 8 + y * 2 + core) * 16 + z * 2 + x_lo


def pairs_of(target, keep=lambda *place: True):
    routes = []
    for section in range(16):
        for dp in range(16):
            place = unpack(section, dp)
            if keep(*place):
                routes.append((pack(*place), pack(*target(*place))))
    return routes


def send(value, target, keep=lambda *place: True):
    return lax.ppermute(value, BOTH, pairs_of(target, keep))


def along_z(value, step):
    return send(value, lambda xh, y, c, z, x: (xh, y, c, (z + step) % 8, x))


def to_core(value):
    return send(value, lambda xh, y, c, z, x: (xh, y, 1 - c, z, x))


def to_y(value):
    return send(value, lambda xh, y, c, z, x: (xh, y ^ 1, c, z, x))


def to_x(value):
    return send(value, lambda xh, y, c, z, x: (xh, y, c, z, 1 - x))


def to_first(value):
    return send(
        value,
        lambda xh, y, c, z, x: (xh, y, c, z, 1 - x) if c == 0 else (xh, y ^ 1, c, z, x),
    )


def to_second(value):
    return send(
        value,
        lambda xh, y, c, z, x: (xh, y ^ 1, c, z, x) if c == 0 else (xh, y, c, z, 1 - x),
    )


def ring(block):
    held = {0: block}
    for step in range(1, 5):
        held[step] = along_z(held[step - 1], 1)
        if step < 4:
            held[-step] = along_z(held[1 - step], -1)
    return held


def neighbourhood(block):
    first = to_first(block)
    second = to_second(block)
    third = to_second(first)
    return jnp.stack([block, first, second, third])


def hop_forward(value, stage):
    if stage == 1:
        return send(
            value,
            lambda xh, y, c, z, x: (1, 3 - y, c, z, 1 - x),
            lambda xh, y, c, z, x: xh == 0 and y >= 2,
        )
    return send(
        value,
        lambda xh, y, c, z, x: (xh, 3 - y, c, z, x),
        lambda xh, y, c, z, x: xh * 2 + y // 2 == stage,
    )


def hop_backward(value, stage):
    if stage == 2:
        return send(
            value,
            lambda xh, y, c, z, x: (0, 3 - y, c, z, 1 - x),
            lambda xh, y, c, z, x: xh == 1 and y < 2,
        )
    return send(
        value,
        lambda xh, y, c, z, x: (xh, 3 - y, c, z, x),
        lambda xh, y, c, z, x: xh * 2 + y // 2 == stage,
    )


def gelu_value(values):
    return 0.5 * values * (1.0 + lax.erf(values * root_half))


def gelu_slope(values):
    return 0.5 * (1.0 + lax.erf(values * root_half)) + values * inv_root_tau * jnp.exp(
        -0.5 * values * values
    )


def where_am_i():
    section = lax.axis_index("section")
    dp = lax.axis_index("dp")
    stage = section // 4
    return stage, (section // 2) % 2, section % 2, dp // 2, dp % 2


def fetch_weights(weight_refs, down, up, down_sem, up_sem, backward):
    _, y_lo, core, z, x_lo = where_am_i()
    down_refs = weight_refs[: 2 * len(GROUPS)]
    up_refs = weight_refs[2 * len(GROUPS) :]

    def one_layer(step, carry):
        layer = LAYERS - 1 - step if backward else step
        parity = layer % 2
        y_far = (layer // 2 + y_lo) % 2

        def start_down(offset):
            for index, distances in enumerate(GROUPS):
                source = down_refs[2 * index + offset]
                for member, distance in enumerate(distances):
                    for x_far in range(2):
                        entry = lax.select(parity == 0, x_far + 2 * y_far, y_far + 2 * x_far)
                        block = ((x_lo + x_far) % 2) * 8 + (z - distance + 8) % 8
                        pltpu.make_async_copy(
                            source.at[entry, member], down.at[layer, block], down_sem.at[layer]
                        ).start()

        def start_up(offset):
            for index, distance in enumerate(SINGLES):
                source = up_refs[2 * index + offset]
                for x_far in range(2):
                    entry = lax.select(parity == 0, x_far + 2 * y_far, y_far + 2 * x_far)
                    block = ((x_lo + x_far) % 2) * 8 + (z - distance + 8) % 8
                    pltpu.make_async_copy(
                        source.at[entry], up.at[layer, block], up_sem.at[layer]
                    ).start()

        @pl.when(parity == core)
        def _():
            if backward:
                start_up(0)
                start_down(0)
            else:
                start_down(0)
                start_up(0)

        @pl.when(parity != core)
        def _():
            if backward:
                start_up(1)
                start_down(1)
            else:
                start_down(1)
                start_up(1)

        return carry

    lax.fori_loop(0, LAYERS, one_layer, 0)


def span(block):
    return slice(block * BLOCK, (block + 1) * BLOCK)


def forward_kernel(stage, aliased, *refs):
    count = 2 * len(GROUPS) + 2 * len(SINGLES)
    h_in = refs[0]
    weight_refs = refs[1 : 1 + count]
    rest = refs[1 + count + (3 if aliased else 0) :]
    h_out, h_save, ua_save, zs_save = rest[:4]
    down, up, hidden, ua, zs, down_sem, up_sem, in_sem, h_sem, ua_sem, zs_sem = rest[4:]

    @pl.when(where_am_i()[0] == stage)
    def _():
        load = pltpu.make_async_copy(h_in, hidden.at[0], in_sem)
        load.start()
        fetch_weights(weight_refs, down, up, down_sem, up_sem, False)
        load.wait()

        def one_layer(layer, carry):
            total = jnp.zeros((ROWS, BLOCK), F32)
            for block in range(BLOCKS):
                part = hidden[layer, :, span(block)].astype(F32)
                total += part * part
            mean = jnp.sum(total, axis=-1, keepdims=True) * (1.0 / WIDTH)
            scaling = lax.rsqrt(mean + epsilon)
            pltpu.make_async_copy(down.at[layer], down.at[layer], down_sem.at[layer]).wait()
            latent = jnp.zeros((ROWS, RANK), F32)
            for block in range(BLOCKS):
                part = hidden[layer, :, span(block)].astype(F32)
                normed = (part * scaling).astype(BF)
                ua[layer, :, span(block)] = normed
                latent += jnp.dot(normed, down[layer, block], preferred_element_type=F32)
            active = gelu_value(latent).astype(BF)
            ua[layer, :, WIDTH:] = active
            zs[layer, :, :RANK] = latent
            zs[layer, :, RANK:] = jnp.broadcast_to(scaling, (ROWS, 128))
            pltpu.make_async_copy(hidden.at[layer], h_save.at[layer], h_sem.at[layer]).start()
            pltpu.make_async_copy(ua.at[layer], ua_save.at[layer], ua_sem.at[layer]).start()
            pltpu.make_async_copy(zs.at[layer], zs_save.at[layer], zs_sem.at[layer]).start()
            pltpu.make_async_copy(up.at[layer], up.at[layer], up_sem.at[layer]).wait()
            for block in range(BLOCKS):
                part = hidden[layer, :, span(block)].astype(F32)
                added = jnp.dot(active, up[layer, block], preferred_element_type=F32)
                hidden[layer + 1, :, span(block)] = (part + added).astype(BF)
            return carry

        lax.fori_loop(0, LAYERS, one_layer, 0)
        last = pltpu.make_async_copy(hidden.at[LAYERS], h_out, in_sem)
        last.start()
        for layer in range(LAYERS):
            pltpu.make_async_copy(hidden.at[layer], h_save.at[layer], h_sem.at[layer]).wait()
            pltpu.make_async_copy(ua.at[layer], ua_save.at[layer], ua_sem.at[layer]).wait()
            pltpu.make_async_copy(zs.at[layer], zs_save.at[layer], zs_sem.at[layer]).wait()
        last.wait()


def backward_kernel(stage, aliased, *refs):
    count = 2 * len(GROUPS) + 2 * len(SINGLES)
    c_in, h_save, zs_save = refs[:3]
    weight_refs = refs[3 : 3 + count]
    rest = refs[3 + count + (1 if aliased else 0) :]
    c_out, cz_save = rest[:2]
    down, up, hidden, cz, zs, down_sem, up_sem, in_sem, cz_sem = rest[2:]
    contract_last = (((1,), (1,)), ((), ()))

    @pl.when(where_am_i()[0] == stage)
    def _():
        loads = [
            pltpu.make_async_copy(c_in, cz.at[LAYERS, :, :WIDTH], in_sem.at[0]),
            pltpu.make_async_copy(zs_save, zs, in_sem.at[1]),
            pltpu.make_async_copy(h_save, hidden, in_sem.at[2]),
        ]
        for load in loads:
            load.start()
        fetch_weights(weight_refs, down, up, down_sem, up_sem, True)
        for load in loads:
            load.wait()

        def one_layer(step, carry):
            layer = LAYERS - 1 - step
            pltpu.make_async_copy(up.at[layer], up.at[layer], up_sem.at[layer]).wait()
            dactive = jnp.zeros((ROWS, RANK), F32)
            for block in range(BLOCKS):
                dactive += lax.dot_general(
                    cz[layer + 1, :, span(block)],
                    up[layer, block],
                    contract_last,
                    preferred_element_type=F32,
                )
            latent = zs[layer, :, :RANK]
            scaling = zs[layer, :, RANK:][:, :1]
            dlatent = (dactive * gelu_slope(latent)).astype(BF)
            cz[layer + 1, :, WIDTH:] = dlatent
            inner = jnp.sum(dlatent.astype(F32) * latent, axis=-1, keepdims=True) * (1.0 / WIDTH)
            pltpu.make_async_copy(cz.at[layer + 1], cz_save.at[layer], cz_sem.at[layer]).start()
            pltpu.make_async_copy(down.at[layer], down.at[layer], down_sem.at[layer]).wait()
            for block in range(BLOCKS):
                unit_grad = lax.dot_general(
                    dlatent, down[layer, block], contract_last, preferred_element_type=F32
                )
                unit_rows = hidden[layer, :, span(block)].astype(F32) * scaling
                passed = cz[layer + 1, :, span(block)].astype(F32) + scaling * (
                    unit_grad - unit_rows * inner
                )
                cz[layer, :, span(block)] = passed.astype(BF)
            return carry

        lax.fori_loop(0, LAYERS, one_layer, 0)
        last = pltpu.make_async_copy(cz.at[0, :, :WIDTH], c_out, in_sem.at[0])
        last.start()
        for layer in range(LAYERS):
            pltpu.make_async_copy(cz.at[layer + 1], cz_save.at[layer], cz_sem.at[layer]).wait()
        last.wait()


def any_specs(number):
    return [pl.BlockSpec(memory_space=pl.ANY)] * number


def weight_scratch():
    return [
        pltpu.VMEM((LAYERS, BLOCKS, BLOCK, RANK), BF),
        pltpu.VMEM((LAYERS, BLOCKS, RANK, BLOCK), BF),
    ]


row_shape = jax.ShapeDtypeStruct((ROWS, WIDTH), BF)
h_shape = jax.ShapeDtypeStruct((LAYERS, ROWS, WIDTH), BF)
pack_shape = jax.ShapeDtypeStruct((LAYERS, ROWS, EXTRA), BF)
zs_shape = jax.ShapeDtypeStruct((LAYERS, ROWS, RANK + 128), F32)
cost = pl.CostEstimate(flops=2 * 10**9, bytes_accessed=40 * 2**20, transcendentals=10**5)


def run_forward(stage, h_in, weights, saved):
    operands = [h_in, *weights, *(saved or ())]
    first = 1 + len(weights)
    return pl.pallas_call(
        functools.partial(forward_kernel, stage, saved is not None),
        out_shape=(row_shape, h_shape, pack_shape, zs_shape),
        in_specs=any_specs(len(operands)),
        out_specs=tuple(any_specs(4)),
        scratch_shapes=[
            *weight_scratch(),
            pltpu.VMEM((LAYERS + 1, ROWS, WIDTH), BF),
            pltpu.VMEM((LAYERS, ROWS, EXTRA), BF),
            pltpu.VMEM((LAYERS, ROWS, RANK + 128), F32),
            pltpu.SemaphoreType.DMA((LAYERS,)),
            pltpu.SemaphoreType.DMA((LAYERS,)),
            pltpu.SemaphoreType.DMA,
            pltpu.SemaphoreType.DMA((LAYERS,)),
            pltpu.SemaphoreType.DMA((LAYERS,)),
            pltpu.SemaphoreType.DMA((LAYERS,)),
        ],
        input_output_aliases={first + i: 1 + i for i in range(3)} if saved else {},
        compiler_params=pltpu.CompilerParams(vmem_limit_bytes=VMEM_LIMIT),
        cost_estimate=cost,
    )(*operands)


def run_backward(stage, c_in, h_save, zs_save, weights, saved):
    operands = [c_in, h_save, zs_save, *weights, *([] if saved is None else [saved])]
    first = 3 + len(weights)
    return pl.pallas_call(
        functools.partial(backward_kernel, stage, saved is not None),
        out_shape=(row_shape, pack_shape),
        in_specs=any_specs(len(operands)),
        out_specs=tuple(any_specs(2)),
        scratch_shapes=[
            *weight_scratch(),
            pltpu.VMEM((LAYERS, ROWS, WIDTH), BF),
            pltpu.VMEM((LAYERS + 1, ROWS, EXTRA), BF),
            pltpu.VMEM((LAYERS, ROWS, RANK + 128), F32),
            pltpu.SemaphoreType.DMA((LAYERS,)),
            pltpu.SemaphoreType.DMA((LAYERS,)),
            pltpu.SemaphoreType.DMA((3,)),
            pltpu.SemaphoreType.DMA((LAYERS,)),
        ],
        input_output_aliases={first: 1} if saved is not None else {},
        compiler_params=pltpu.CompilerParams(vmem_limit_bytes=VMEM_LIMIT),
        cost_estimate=cost,
    )(*operands)


def gather_weights(down_shard, up_shard):
    up_ring = ring(neighbourhood(up_shard))
    down_ring = ring(down_shard)
    weights = []
    for distances in GROUPS:
        full = neighbourhood(jnp.stack([down_ring[k] for k in distances]))
        weights += [full, to_core(full)]
    for distance in SINGLES:
        weights += [up_ring[distance], to_core(up_ring[distance])]
    return weights


def pick(value, index):
    return lax.dynamic_index_in_dim(value, index, 0, keepdims=False)


def exchange(saved, y_lo, core, x_lo):
    by_core = saved.reshape(2, 2, ROWS, EXTRA).swapaxes(0, 1)
    rows = jnp.concatenate(
        [pick(by_core, core), to_core(pick(by_core, 1 - core))], axis=1
    )
    rows = jnp.concatenate([pick(rows, y_lo), to_y(pick(rows, 1 - y_lo))], axis=0)
    wide = rows[:, :WIDTH].reshape(4 * ROWS, 2, WIDTH // 2).swapaxes(0, 1)
    narrow = rows[:, WIDTH:]
    own = jnp.concatenate([pick(wide, x_lo), narrow], axis=1)
    other = jnp.concatenate([pick(wide, 1 - x_lo), narrow], axis=1)
    rows = jnp.concatenate([own, to_x(other)], axis=0)
    return rows[:, : WIDTH // 2], rows[:, WIDTH // 2 :]


def body(entering, cotangent, down_proj, up_proj):
    section = lax.axis_index("section")
    dp = lax.axis_index("dp")
    y_lo, core, x_lo = (section // 2) % 2, section % 2, dp % 2

    def own_rows(array, half):
        chosen = pick(array, core).reshape(2, ROWS, 8, 2, BLOCK)
        return pick(chosen, half).swapaxes(1, 2).reshape(ROWS, WIDTH)

    hidden = own_rows(entering, y_lo)
    incoming = send(
        own_rows(cotangent, 1 - y_lo),
        lambda xh, y, c, z, x: (xh, y, c, z, 1 - x),
        lambda xh, y, c, z, x: xh == 1 and y >= 2,
    )
    weights = gather_weights(down_proj[0], up_proj[0])

    saved = None
    for stage in range(4):
        hidden, *saved = run_forward(stage, hidden, weights, saved)
        if stage < 3:
            hidden = hop_forward(hidden, stage)
    h_save, ua_save, zs_save = saved

    cz_save = None
    for stage in (3, 2, 1, 0):
        incoming, cz_save = run_backward(stage, incoming, h_save, zs_save, weights, cz_save)
        if stage > 0:
            incoming = hop_backward(incoming, stage)

    normed, active = exchange(ua_save, y_lo, core, x_lo)
    cotangents, dlatent = exchange(cz_save, y_lo, core, x_lo)
    contract_rows = (((0,), (0,)), ((), ()))
    pieces = jnp.concatenate(
        [
            lax.dot_general(normed, dlatent, contract_rows, preferred_element_type=F32),
            lax.dot_general(cotangents, active, contract_rows, preferred_element_type=F32),
        ],
        axis=1,
    ).astype(BF)
    groups = [[x + 2 * z for z in range(8)] for x in range(2)]
    totals = lax.psum_scatter(
        pieces, "dp", scatter_dimension=0, axis_index_groups=groups, tiled=True
    ).astype(F32)
    return (totals[:, :RANK][None], totals[:, RANK:].T[None])


def solution(mesh):
    return jax.shard_map(
        body,
        mesh=mesh,
        in_specs=(
            P(None, None, "dp", None),
            P(None, None, "dp", None),
            P("section", "dp", None),
            P("section", None, "dp"),
        ),
        out_specs=(P("section", "dp", None), P("section", None, "dp")),
        check_vma=False,
    )
```

```python
import functools

import jax
import jax.numpy as jnp
from jax import lax
from jax.experimental import pallas as pl
from jax.experimental.pallas import tpu as pltpu
from jax.sharding import PartitionSpec as P

epsilon = 1e-05
root_half = 0.7071067811865476
inv_root_tau = 0.3989422804014327

BF = jnp.bfloat16
F32 = jnp.float32
BOTH = ("section", "dp")
WIDTH = 8192
RANK = 256
BLOCK = 512
BLOCKS = WIDTH // BLOCK
ROWS = 32
LAYERS = 4
HALF = WIDTH // 2
PACKED = HALF + RANK
MINOR = 48
MAJOR = RANK - MINOR
VMEM_LIMIT = 12 * 2**20
FIRST_LIMIT = 25 * 2**20

def unpack(section, dp):
    return section // 8, (section // 2) % 4, section % 2, dp // 2, dp % 2


def pack(x_hi, y, core, z, x_lo):
    return (x_hi * 8 + y * 2 + core) * 16 + z * 2 + x_lo


def pairs_of(target, keep=lambda *place: True):
    routes = []
    for section in range(16):
        for dp in range(16):
            place = unpack(section, dp)
            if keep(*place):
                routes.append((pack(*place), pack(*target(*place))))
    return routes


def send(value, target, keep=lambda *place: True):
    return lax.ppermute(value, BOTH, pairs_of(target, keep))


def along_z(value, step):
    return send(value, lambda xh, y, c, z, x: (xh, y, c, (z + step) % 8, x))


def to_core(value):
    return send(value, lambda xh, y, c, z, x: (xh, y, 1 - c, z, x))


def to_y(value):
    return send(value, lambda xh, y, c, z, x: (xh, y ^ 1, c, z, x))


def to_x(value):
    return send(value, lambda xh, y, c, z, x: (xh, y, c, z, 1 - x))


def to_first(value):
    return send(
        value,
        lambda xh, y, c, z, x: (xh, y, c, z, 1 - x) if c == 0 else (xh, y ^ 1, c, z, x),
    )


def to_second(value):
    return send(
        value,
        lambda xh, y, c, z, x: (xh, y ^ 1, c, z, x) if c == 0 else (xh, y, c, z, 1 - x),
    )


def exchange_pair(block):
    first = to_first(block)
    second = to_second(block)
    third = to_second(first)
    return jnp.stack([block, first, second, third])


def noop_kernel(*refs):
    pass


def after(value, *needed):
    return pl.pallas_call(
        noop_kernel,
        out_shape=jax.ShapeDtypeStruct(value.shape, value.dtype),
        in_specs=any_specs(1 + len(needed)),
        out_specs=pl.BlockSpec(memory_space=pltpu.HBM),
        input_output_aliases={0: 0},
        compiler_params=pltpu.CompilerParams(vmem_limit_bytes=VMEM_LIMIT),
    )(value, *needed)


def hop_forward(value, stage):
    if stage == 1:
        return send(
            value,
            lambda xh, y, c, z, x: (1, 3 - y, c, z, 1 - x),
            lambda xh, y, c, z, x: xh == 0 and y >= 2,
        )
    return send(
        value,
        lambda xh, y, c, z, x: (xh, 3 - y, c, z, x),
        lambda xh, y, c, z, x: xh * 2 + y // 2 == stage,
    )


def hop_backward(value, stage):
    if stage == 2:
        return send(
            value,
            lambda xh, y, c, z, x: (0, 3 - y, c, z, 1 - x),
            lambda xh, y, c, z, x: xh == 1 and y < 2,
        )
    return send(
        value,
        lambda xh, y, c, z, x: (xh, 3 - y, c, z, x),
        lambda xh, y, c, z, x: xh * 2 + y // 2 == stage,
    )


def gelu_value(values):
    return 0.5 * values * (1.0 + lax.erf(values * root_half))


def gelu_slope(values):
    return 0.5 * (1.0 + lax.erf(values * root_half)) + values * inv_root_tau * jnp.exp(
        -0.5 * values * values
    )


def where_am_i():
    section = lax.axis_index("section")
    dp = lax.axis_index("dp")
    stage = section // 4
    return stage, (section // 2) % 2, section % 2, dp // 2, dp % 2


def span(block):
    return slice(block * BLOCK, (block + 1) * BLOCK)


def fetch(plan, sources, down, up, down_sem, up_sem):
    _, y_lo, core, z, x_lo = where_am_i()

    def copies(layer, offset):
        parity = layer % 2
        y_far = (layer // 2 + y_lo) % 2
        downs, ups = [], []
        for index, (kind, distances) in enumerate(plan):
            source = sources[2 * index + offset]
            for member, distance in enumerate(distances):
                for x_far in range(2):
                    entry = lax.select(parity == 0, x_far + 2 * y_far, y_far + 2 * x_far)
                    block = ((x_lo + x_far) % 2) * 8 + (z - distance + 8) % 8
                    if kind == "both":
                        downs.append(
                            (source.at[entry, member, pl.ds(0, BLOCK)], down.at[layer, block])
                        )
                        for side in range(2):
                            rows = pl.ds(BLOCK + side * MINOR, MINOR)
                            columns = pl.ds(side * RANK, RANK)
                            ups.append(
                                (
                                    source.at[entry, member, rows],
                                    up.at[layer, block, pl.ds(MAJOR, MINOR), columns],
                                )
                            )
                    else:
                        low, high = kind
                        ups.append(
                            (source.at[entry], up.at[layer, block, pl.ds(low, high - low)])
                        )
        return [pltpu.make_async_copy(a, b, down_sem.at[layer]) for a, b in downs] + [
            pltpu.make_async_copy(a, b, up_sem.at[layer]) for a, b in ups
        ]

    def one_layer(layer, carry):
        for offset in range(2):

            @pl.when((layer % 2 == core) == (offset == 0))
            def _():
                for copy in copies(layer, offset):
                    copy.start()

        return carry

    lax.fori_loop(0, LAYERS, one_layer, 0)


def fetched(layer, matrix, sem):
    pltpu.make_async_copy(matrix.at[layer], matrix.at[layer], sem.at[layer]).wait()


down_shape = (LAYERS, BLOCKS, BLOCK, RANK)
up_shape = (LAYERS, BLOCKS, RANK, BLOCK)


def in_vmem(number):
    return [pl.BlockSpec(memory_space=pltpu.VMEM)] * number


def any_specs(number):
    return [pl.BlockSpec(memory_space=pltpu.HBM)] * number


def pack_kernel(parts, *refs):
    sources, (target, sem) = refs[: len(parts)], refs[len(parts) :]
    copies = []
    row = 0
    for index, (source, (place, count)) in enumerate(zip(sources, parts)):
        copies.append(
            pltpu.make_async_copy(
                source.at[place], target.at[pl.ds(row, count)], sem.at[index]
            )
        )
        row += count
    for copy in copies:
        copy.start()
    for copy in copies:
        copy.wait()


def packed_rows(*parts):
    arrays = [array for array, _ in parts]
    takes = [(place, array[place].shape[0]) for array, place in parts]
    shape = (sum(count for _, count in takes), *arrays[0][parts[0][1]].shape[1:])
    return pl.pallas_call(
        functools.partial(pack_kernel, takes),
        out_shape=jax.ShapeDtypeStruct(shape, BF),
        in_specs=any_specs(len(arrays)),
        out_specs=any_specs(1)[0],
        scratch_shapes=[pltpu.SemaphoreType.DMA((len(arrays),))],
        compiler_params=pltpu.CompilerParams(vmem_limit_bytes=4 * 2**20),
    )(*arrays)


def scatter(layer, wide, narrow, kept, sent, sem):
    _, y_lo, core, _, x_lo = where_am_i()
    parity = layer % 2
    y_far = (layer // 2 + y_lo) % 2

    def copies(target):
        made = []
        for half in range(2):
            x_far = (half + x_lo) % 2
            first = lax.select(parity == 0, x_far, y_far)
            second = lax.select(parity == 0, y_far, x_far)
            place = target.at[first, second]
            made.append((wide.at[:, half * HALF : (half + 1) * HALF], place.at[:, :HALF]))
            made.append((narrow, place.at[:, HALF:]))
        return [pltpu.make_async_copy(a, b, sem.at[i]) for i, (a, b) in enumerate(made)]

    def start():
        @pl.when(parity == core)
        def _():
            for copy in copies(kept):
                copy.start()

        @pl.when(parity != core)
        def _():
            for copy in copies(sent):
                copy.start()

    def wait():
        for copy in copies(kept):
            copy.wait()

    return start, wait


def first_kernel(plan, *refs):
    h_in, sources = refs[0], refs[1 : 1 + 2 * len(plan)]
    down, up, *rest = refs[1 + 2 * len(plan) :]
    *rest, down_sem, up_sem = rest
    fetch(plan, sources, down, up, down_sem, up_sem)
    compute_forward(
        0,
        h_in,
        down,
        up,
        *rest,
        ready=lambda layer: fetched(layer, down, down_sem),
        ready_up=lambda layer: fetched(layer, up, up_sem),
    )

    @pl.when(where_am_i()[0] != 0)
    def _():
        for layer in range(LAYERS):
            fetched(layer, down, down_sem)
            fetched(layer, up, up_sem)


def forward_kernel(stage, *refs):
    compute_forward(stage, *refs[:3], *refs[7:])


def compute_forward(
    stage,
    h_in,
    down,
    up,
    h_out,
    hidden,
    zs,
    kept,
    sent,
    normed_rows,
    active_rows,
    sem,
    ready=lambda layer: None,
    ready_up=lambda layer: None,
):
    @pl.when(where_am_i()[0] == stage)
    def _():
        hidden[0] = h_in[...]

        def one_layer(layer, carry):
            total = jnp.zeros((ROWS, BLOCK), F32)
            for block in range(BLOCKS):
                part = hidden[layer, :, span(block)].astype(F32)
                total += part * part
            mean = jnp.sum(total, axis=-1, keepdims=True) * (1.0 / WIDTH)
            scaling = lax.rsqrt(mean + epsilon)
            ready(layer)
            latent = jnp.zeros((ROWS, RANK), F32)
            for block in range(BLOCKS):
                part = hidden[layer, :, span(block)].astype(F32)
                normed = (part * scaling).astype(BF)
                normed_rows[layer, :, span(block)] = normed
                latent += jnp.dot(normed, down[layer, block], preferred_element_type=F32)
            active = gelu_value(latent).astype(BF)
            active_rows[layer] = active
            zs[layer, :, :RANK] = latent
            zs[layer, :, RANK:] = jnp.broadcast_to(scaling, (ROWS, 128))
            start, _ = scatter(
                layer, normed_rows.at[layer], active_rows.at[layer], kept, sent, sem.at[layer]
            )
            start()
            ready_up(layer)

            def passed_on(store):
                for block in range(BLOCKS):
                    part = hidden[layer, :, span(block)].astype(F32)
                    added = jnp.dot(active, up[layer, block], preferred_element_type=F32)
                    store(span(block), (part + added).astype(BF))

            def store_next(columns, value):
                hidden[layer + 1, :, columns] = value

            def store_last(columns, value):
                h_out[:, columns] = value

            @pl.when(layer < LAYERS - 1)
            def _():
                passed_on(store_next)

            @pl.when(layer == LAYERS - 1)
            def _():
                passed_on(store_last)

            return carry

        lax.fori_loop(0, LAYERS, one_layer, 0)

        def one_wait(layer, carry):
            _, wait = scatter(
                layer, normed_rows.at[layer], active_rows.at[layer], kept, sent, sem.at[layer]
            )
            wait()
            return carry

        lax.fori_loop(0, LAYERS, one_wait, 0)


def backward_kernel(stage, aliased, passes, *refs):
    c_in, hidden, zs, down, up = refs[:5]
    rest = refs[5 + (2 if aliased else 0) + passes :]
    c_out, kept, sent = rest[:3]
    cotangent, dlatent_rows, sem = rest[-3:]
    contract_last = (((1,), (1,)), ((), ()))

    @pl.when(where_am_i()[0] == stage)
    def _():
        cotangent[LAYERS - 1] = c_in[...]

        def one_layer(step, carry):
            layer = LAYERS - 1 - step
            dactive = jnp.zeros((ROWS, RANK), F32)
            for block in range(BLOCKS):
                dactive += lax.dot_general(
                    cotangent[layer, :, span(block)],
                    up[layer, block],
                    contract_last,
                    preferred_element_type=F32,
                )
            latent = zs[layer, :, :RANK]
            scaling = zs[layer, :, RANK:][:, :1]
            dlatent = (dactive * gelu_slope(latent)).astype(BF)
            dlatent_rows[layer] = dlatent
            inner = jnp.sum(dlatent.astype(F32) * latent, axis=-1, keepdims=True) * (1.0 / WIDTH)
            start, _ = scatter(
                layer, cotangent.at[layer], dlatent_rows.at[layer], kept, sent, sem.at[layer]
            )
            start()

            def passed_on(store):
                for block in range(BLOCKS):
                    unit_grad = lax.dot_general(
                        dlatent, down[layer, block], contract_last, preferred_element_type=F32
                    )
                    unit_rows = hidden[layer, :, span(block)].astype(F32) * scaling
                    passed = cotangent[layer, :, span(block)].astype(F32) + scaling * (
                        unit_grad - unit_rows * inner
                    )
                    store(span(block), passed.astype(BF))

            def store_next(columns, value):
                cotangent[layer - 1, :, columns] = value

            def store_last(columns, value):
                c_out[:, columns] = value

            @pl.when(layer > 0)
            def _():
                passed_on(store_next)

            @pl.when(layer == 0)
            def _():
                passed_on(store_last)

            return carry

        lax.fori_loop(0, LAYERS, one_layer, 0)

        def one_wait(layer, carry):
            _, wait = scatter(
                layer, cotangent.at[layer], dlatent_rows.at[layer], kept, sent, sem.at[layer]
            )
            wait()
            return carry

        lax.fori_loop(0, LAYERS, one_wait, 0)


row_shape = jax.ShapeDtypeStruct((ROWS, WIDTH), BF)
side_shape = pltpu.HBM((2, 2, ROWS, PACKED), BF)
cost = pl.CostEstimate(flops=2 * 10**9, bytes_accessed=40 * 2**20, transcendentals=10**5)


saved_shapes = (
    pltpu.VMEM((LAYERS, ROWS, WIDTH), BF),
    pltpu.VMEM((LAYERS, ROWS, RANK + 128), F32),
    side_shape,
    side_shape,
)


def row_scratch():
    return [
        pltpu.VMEM((LAYERS, ROWS, WIDTH), BF),
        pltpu.VMEM((LAYERS, ROWS, RANK), BF),
        pltpu.SemaphoreType.DMA((LAYERS, 4)),
    ]


def run_first(h_in, entries):
    plan = tuple(what for what, *_ in entries)
    operands = [h_in] + [array for _, *pair in entries for array in pair]
    down, up, h_out, *saved = pl.pallas_call(
        functools.partial(first_kernel, plan),
        out_shape=(
            pltpu.VMEM(down_shape, BF),
            pltpu.VMEM(up_shape, BF),
            row_shape,
            *saved_shapes,
        ),
        in_specs=in_vmem(1) + any_specs(len(operands) - 1),
        out_specs=tuple(in_vmem(5) + any_specs(2)),
        scratch_shapes=[
            *row_scratch(),
            pltpu.SemaphoreType.DMA((LAYERS,)),
            pltpu.SemaphoreType.DMA((LAYERS,)),
        ],
        compiler_params=pltpu.CompilerParams(vmem_limit_bytes=FIRST_LIMIT),
        cost_estimate=cost,
    )(*operands)
    return (down, up), h_out, saved


def run_forward(stage, h_in, weights, saved):
    return pl.pallas_call(
        functools.partial(forward_kernel, stage),
        out_shape=(row_shape, *saved_shapes),
        in_specs=in_vmem(5) + any_specs(2),
        out_specs=tuple(in_vmem(3) + any_specs(2)),
        scratch_shapes=row_scratch(),
        input_output_aliases={3 + i: 1 + i for i in range(4)},
        compiler_params=pltpu.CompilerParams(vmem_limit_bytes=VMEM_LIMIT),
        cost_estimate=cost,
    )(h_in, *weights, *saved)


def run_backward(stage, c_in, hidden, zs, weights, saved, passed=()):
    operands = [c_in, hidden, zs, *weights, *(saved or ()), *passed]
    first = 5 + len(saved or ())
    aliases = {5: 1, 6: 2} if saved else {}
    aliases.update({first + i: 3 + i for i in range(len(passed))})
    return pl.pallas_call(
        functools.partial(backward_kernel, stage, saved is not None, len(passed)),
        out_shape=(
            row_shape,
            side_shape,
            side_shape,
            *[jax.ShapeDtypeStruct(p.shape, p.dtype) for p in passed],
        ),
        in_specs=in_vmem(5) + any_specs(first - 5 + len(passed)),
        out_specs=tuple(in_vmem(1) + any_specs(2 + len(passed))),
        scratch_shapes=[
            pltpu.VMEM((LAYERS, ROWS, WIDTH), BF),
            pltpu.VMEM((LAYERS, ROWS, RANK), BF),
            pltpu.SemaphoreType.DMA((LAYERS, 4)),
        ],
        input_output_aliases=aliases,
        compiler_params=pltpu.CompilerParams(vmem_limit_bytes=VMEM_LIMIT),
        cost_estimate=cost,
    )(*operands)


def ring(block):
    held = {0: block}
    for step in range(1, 5):
        held[step] = along_z(held[step - 1], 1)
        if step < 4:
            held[-step] = along_z(held[1 - step], -1)
    return held


def gather_weights(down_shard, up_shard, needed):
    minor = up_shard[MAJOR:]
    packed = jnp.concatenate([down_shard, minor[:, :RANK], minor[:, RANK:]], axis=0)
    major = ring(exchange_pair(up_shard[:MAJOR]))
    small = ring(packed)
    entries = []
    for members in ((0,), (1, -1), (2, -2), (3, -3), (4,)):
        block = jnp.stack([small[k] for k in members])
        if members[0] == 2:
            block = after(block, *needed)
        full = exchange_pair(block)
        entries.append((("both", members), full, to_core(full)))
    for k in (0, 1, -1, 2, -2, 3, -3, 4):
        entries.append((((0, MAJOR), (k,)), major[k], to_core(major[k])))
    return entries


def exchange(kept, sent):
    other = to_core(sent)
    near = to_first(packed_rows((kept, (1,))))
    far = to_first(packed_rows((other, (1,))))
    outgoing = packed_rows((kept, (0, 1)), (other, (0, 1)), (near, (1,)), (far, (1,)))
    arrived = to_second(outgoing)
    return packed_rows(
        (kept, (0, 0)),
        (other, (0, 0)),
        (near, (0,)),
        (far, (0,)),
        (arrived, ()),
    )


def pick(value, index):
    return lax.dynamic_index_in_dim(value, index, 0, keepdims=False)


def body(entering, cotangent, down_proj, up_proj):
    section = lax.axis_index("section")
    y_lo, core = (section // 2) % 2, section % 2

    def own_rows(array, half):
        chosen = pick(array, core).reshape(2, ROWS, 8, 2, BLOCK)
        return pick(chosen, half).swapaxes(1, 2).reshape(ROWS, WIDTH)

    hidden = own_rows(entering, y_lo)
    seeds = own_rows(cotangent, 1 - y_lo)
    entries = gather_weights(down_proj[0], up_proj[0], (hidden, seeds))

    weights, hidden, saved = run_first(hidden, entries)
    incoming = send(
        after(seeds, saved[2]),
        lambda xh, y, c, z, x: (xh, y, c, z, 1 - x),
        lambda xh, y, c, z, x: xh == 1 and y >= 2,
    )
    for stage in range(4):
        if stage > 0:
            hidden, *saved = run_forward(stage, hidden, weights, saved)
        if stage < 3:
            hidden = hop_forward(hidden, stage)
    h_save, zs_save, *sides = saved

    saved = None
    for stage in (3, 2, 1, 0):
        passed = ()
        if stage == 1:
            passed = sides
        if stage == 0:
            passed = (normed,)
        incoming, *saved = run_backward(
            stage, incoming, h_save, zs_save, weights, saved, passed
        )
        saved, passed = saved[:2], saved[2:]
        if stage > 0:
            incoming = hop_backward(incoming, stage)
        if stage == 1:
            normed = exchange(*passed)
    normed = passed[0]
    cotangents = exchange(*saved)

    contract_rows = (((0,), (0,)), ((), ()))

    def partial(wide, narrow):
        return lax.dot_general(
            wide[:, :HALF], narrow[:, HALF:], contract_rows, preferred_element_type=F32
        )

    pieces = jnp.concatenate([partial(normed, cotangents), partial(cotangents, normed)], axis=1)
    groups = [[x + 2 * z for z in range(8)] for x in range(2)]
    totals = lax.psum_scatter(
        pieces.astype(BF), "dp", scatter_dimension=0, axis_index_groups=groups, tiled=True
    ).astype(F32)
    return (totals[:, :RANK][None], totals[:, RANK:].T[None])


def solution(mesh):
    return jax.shard_map(
        body,
        mesh=mesh,
        in_specs=(
            P(None, None, "dp", None),
            P(None, None, "dp", None),
            P("section", "dp", None),
            P("section", None, "dp"),
        ),
        out_specs=(P("section", "dp", None), P("section", None, "dp")),
        check_vma=False,
    )
```

```python
import functools

import jax
import jax.numpy as jnp
from jax import lax
from jax.experimental import pallas as pl
from jax.experimental.pallas import tpu as pltpu
from jax.sharding import PartitionSpec as P

epsilon = 1e-05
root_half = 0.7071067811865476
inv_root_tau = 0.3989422804014327

BF = jnp.bfloat16
F32 = jnp.float32
BOTH = ("section", "dp")
WIDTH = 8192
RANK = 256
BLOCK = 512
BLOCKS = WIDTH // BLOCK
ROWS = 32
LAYERS = 4
HALF = WIDTH // 2
PACKED = HALF + RANK
MINOR = 48
MAJOR = RANK - MINOR
VMEM_LIMIT = 12 * 2**20
FIRST_LIMIT = 25 * 2**20

def unpack(section, dp):
    return section // 8, (section // 2) % 4, section % 2, dp // 2, dp % 2


def pack(x_hi, y, core, z, x_lo):
    return (x_hi * 8 + y * 2 + core) * 16 + z * 2 + x_lo


def pairs_of(target, keep=lambda *place: True):
    routes = []
    for section in range(16):
        for dp in range(16):
            place = unpack(section, dp)
            if keep(*place):
                routes.append((pack(*place), pack(*target(*place))))
    return routes


def send(value, target, keep=lambda *place: True):
    return lax.ppermute(value, BOTH, pairs_of(target, keep))


def along_z(value, step):
    return send(value, lambda xh, y, c, z, x: (xh, y, c, (z + step) % 8, x))


def to_core(value):
    return send(value, lambda xh, y, c, z, x: (xh, y, 1 - c, z, x))


def to_y(value):
    return send(value, lambda xh, y, c, z, x: (xh, y ^ 1, c, z, x))


def to_x(value):
    return send(value, lambda xh, y, c, z, x: (xh, y, c, z, 1 - x))


def to_first(value):
    return send(
        value,
        lambda xh, y, c, z, x: (xh, y, c, z, 1 - x) if c == 0 else (xh, y ^ 1, c, z, x),
    )


def to_second(value):
    return send(
        value,
        lambda xh, y, c, z, x: (xh, y ^ 1, c, z, x) if c == 0 else (xh, y, c, z, 1 - x),
    )


def exchange_pair(block):
    first = to_first(block)
    second = to_second(block)
    third = to_second(first)
    return jnp.stack([block, first, second, third])


def noop_kernel(*refs):
    pass


def after(value, *needed):
    return pl.pallas_call(
        noop_kernel,
        out_shape=jax.ShapeDtypeStruct(value.shape, value.dtype),
        in_specs=any_specs(1 + len(needed)),
        out_specs=pl.BlockSpec(memory_space=pltpu.HBM),
        input_output_aliases={0: 0},
        compiler_params=pltpu.CompilerParams(vmem_limit_bytes=VMEM_LIMIT),
    )(value, *needed)


def hop_forward(value, stage):
    if stage == 1:
        return send(
            value,
            lambda xh, y, c, z, x: (1, 3 - y, c, z, 1 - x),
            lambda xh, y, c, z, x: xh == 0 and y >= 2,
        )
    return send(
        value,
        lambda xh, y, c, z, x: (xh, 3 - y, c, z, x),
        lambda xh, y, c, z, x: xh * 2 + y // 2 == stage,
    )


def hop_backward(value, stage):
    if stage == 2:
        return send(
            value,
            lambda xh, y, c, z, x: (0, 3 - y, c, z, 1 - x),
            lambda xh, y, c, z, x: xh == 1 and y < 2,
        )
    return send(
        value,
        lambda xh, y, c, z, x: (xh, 3 - y, c, z, x),
        lambda xh, y, c, z, x: xh * 2 + y // 2 == stage,
    )


def gelu_value(values):
    return 0.5 * values * (1.0 + lax.erf(values * root_half))


def gelu_slope(values):
    return 0.5 * (1.0 + lax.erf(values * root_half)) + values * inv_root_tau * jnp.exp(
        -0.5 * values * values
    )


def where_am_i():
    section = lax.axis_index("section")
    dp = lax.axis_index("dp")
    stage = section // 4
    return stage, (section // 2) % 2, section % 2, dp // 2, dp % 2


def span(block):
    return slice(block * BLOCK, (block + 1) * BLOCK)


def fetch(plan, sources, down, up, down_sem, up_sem):
    _, y_lo, core, z, x_lo = where_am_i()

    def copies(layer, offset):
        parity = layer % 2
        y_far = (layer // 2 + y_lo) % 2
        downs, ups = [], []
        for index, (kind, distances) in enumerate(plan):
            source = sources[2 * index + offset]
            for member, distance in enumerate(distances):
                for x_far in range(2):
                    entry = lax.select(parity == 0, x_far + 2 * y_far, y_far + 2 * x_far)
                    block = ((x_lo + x_far) % 2) * 8 + (z - distance + 8) % 8
                    if kind == "both":
                        downs.append(
                            (source.at[entry, member, pl.ds(0, BLOCK)], down.at[layer, block])
                        )
                        for side in range(2):
                            rows = pl.ds(BLOCK + side * MINOR, MINOR)
                            columns = pl.ds(side * RANK, RANK)
                            ups.append(
                                (
                                    source.at[entry, member, rows],
                                    up.at[layer, block, pl.ds(MAJOR, MINOR), columns],
                                )
                            )
                    else:
                        low, high = kind
                        ups.append(
                            (source.at[entry], up.at[layer, block, pl.ds(low, high - low)])
                        )
        return [pltpu.make_async_copy(a, b, down_sem.at[layer]) for a, b in downs] + [
            pltpu.make_async_copy(a, b, up_sem.at[layer]) for a, b in ups
        ]

    def one_layer(layer, carry):
        for offset in range(2):

            @pl.when((layer % 2 == core) == (offset == 0))
            def _():
                for copy in copies(layer, offset):
                    copy.start()

        return carry

    lax.fori_loop(0, LAYERS, one_layer, 0)


def fetched(layer, matrix, sem):
    pltpu.make_async_copy(matrix.at[layer], matrix.at[layer], sem.at[layer]).wait()


down_shape = (LAYERS, BLOCKS, BLOCK, RANK)
up_shape = (LAYERS, BLOCKS, RANK, BLOCK)


def in_vmem(number):
    return [pl.BlockSpec(memory_space=pltpu.VMEM)] * number


def any_specs(number):
    return [pl.BlockSpec(memory_space=pltpu.HBM)] * number


def pack_kernel(parts, *refs):
    sources, (target, sem) = refs[: len(parts)], refs[len(parts) :]
    copies = []
    row = 0
    for index, (source, (place, count)) in enumerate(zip(sources, parts)):
        copies.append(
            pltpu.make_async_copy(
                source.at[place], target.at[pl.ds(row, count)], sem.at[index]
            )
        )
        row += count
    for copy in copies:
        copy.start()
    for copy in copies:
        copy.wait()


def packed_rows(*parts):
    arrays = [array for array, _ in parts]
    takes = [(place, array[place].shape[0]) for array, place in parts]
    shape = (sum(count for _, count in takes), *arrays[0][parts[0][1]].shape[1:])
    return pl.pallas_call(
        functools.partial(pack_kernel, takes),
        out_shape=jax.ShapeDtypeStruct(shape, BF),
        in_specs=any_specs(len(arrays)),
        out_specs=any_specs(1)[0],
        scratch_shapes=[pltpu.SemaphoreType.DMA((len(arrays),))],
        compiler_params=pltpu.CompilerParams(vmem_limit_bytes=4 * 2**20),
    )(*arrays)


def scatter(layer, wide, narrow, kept, sent, sem):
    _, y_lo, core, _, x_lo = where_am_i()
    parity = layer % 2
    y_far = (layer // 2 + y_lo) % 2

    def copies(target):
        made = []
        for half in range(2):
            x_far = (half + x_lo) % 2
            first = lax.select(parity == 0, x_far, y_far)
            second = lax.select(parity == 0, y_far, x_far)
            place = target.at[first, second]
            made.append((wide.at[:, half * HALF : (half + 1) * HALF], place.at[:, :HALF]))
            made.append((narrow, place.at[:, HALF:]))
        return [pltpu.make_async_copy(a, b, sem.at[i]) for i, (a, b) in enumerate(made)]

    def start():
        @pl.when(parity == core)
        def _():
            for copy in copies(kept):
                copy.start()

        @pl.when(parity != core)
        def _():
            for copy in copies(sent):
                copy.start()

    def wait():
        for copy in copies(kept):
            copy.wait()

    return start, wait


def first_kernel(plan, *refs):
    h_in, sources = refs[0], refs[1 : 1 + 2 * len(plan)]
    down, up, *rest = refs[1 + 2 * len(plan) :]
    *rest, down_sem, up_sem = rest
    fetch(plan, sources, down, up, down_sem, up_sem)
    compute_forward(
        0,
        h_in,
        down,
        up,
        *rest,
        ready=lambda layer: fetched(layer, down, down_sem),
        ready_up=lambda layer: fetched(layer, up, up_sem),
    )

    @pl.when(where_am_i()[0] != 0)
    def _():
        for layer in range(LAYERS):
            fetched(layer, down, down_sem)
            fetched(layer, up, up_sem)


def forward_kernel(stage, *refs):
    compute_forward(stage, *refs[:3], *refs[7:])


def compute_forward(
    stage,
    h_in,
    down,
    up,
    h_out,
    hidden,
    zs,
    kept,
    sent,
    normed_rows,
    active_rows,
    sem,
    ready=lambda layer: None,
    ready_up=lambda layer: None,
):
    @pl.when(where_am_i()[0] == stage)
    def _():
        hidden[0] = h_in[...]

        def one_layer(layer, carry):
            total = jnp.zeros((ROWS, BLOCK), F32)
            for block in range(BLOCKS):
                part = hidden[layer, :, span(block)].astype(F32)
                total += part * part
            mean = jnp.sum(total, axis=-1, keepdims=True) * (1.0 / WIDTH)
            scaling = lax.rsqrt(mean + epsilon)
            ready(layer)
            latent = jnp.zeros((ROWS, RANK), F32)
            for block in range(BLOCKS):
                part = hidden[layer, :, span(block)].astype(F32)
                normed = (part * scaling).astype(BF)
                normed_rows[layer, :, span(block)] = normed
                latent += jnp.dot(normed, down[layer, block], preferred_element_type=F32)
            active = gelu_value(latent).astype(BF)
            active_rows[layer] = active
            zs[layer, :, :RANK] = latent
            zs[layer, :, RANK:] = jnp.broadcast_to(scaling, (ROWS, 128))
            start, _ = scatter(
                layer, normed_rows.at[layer], active_rows.at[layer], kept, sent, sem.at[layer]
            )
            start()
            ready_up(layer)

            def passed_on(store):
                for block in range(BLOCKS):
                    part = hidden[layer, :, span(block)].astype(F32)
                    added = jnp.dot(active, up[layer, block], preferred_element_type=F32)
                    store(span(block), (part + added).astype(BF))

            def store_next(columns, value):
                hidden[layer + 1, :, columns] = value

            def store_last(columns, value):
                h_out[:, columns] = value

            @pl.when(layer < LAYERS - 1)
            def _():
                passed_on(store_next)

            @pl.when(layer == LAYERS - 1)
            def _():
                passed_on(store_last)

            return carry

        lax.fori_loop(0, LAYERS, one_layer, 0)

        def one_wait(layer, carry):
            _, wait = scatter(
                layer, normed_rows.at[layer], active_rows.at[layer], kept, sent, sem.at[layer]
            )
            wait()
            return carry

        lax.fori_loop(0, LAYERS, one_wait, 0)


def backward_kernel(stage, aliased, passes, *refs):
    c_in, hidden, zs, down, up = refs[:5]
    rest = refs[5 + (2 if aliased else 0) + passes :]
    c_out, kept, sent = rest[:3]
    cotangent, dlatent_rows, sem = rest[-3:]
    contract_last = (((1,), (1,)), ((), ()))

    @pl.when(where_am_i()[0] == stage)
    def _():
        cotangent[LAYERS - 1] = c_in[...]

        def one_layer(step, carry):
            layer = LAYERS - 1 - step
            dactive = jnp.zeros((ROWS, RANK), F32)
            for block in range(BLOCKS):
                dactive += lax.dot_general(
                    cotangent[layer, :, span(block)],
                    up[layer, block],
                    contract_last,
                    preferred_element_type=F32,
                )
            latent = zs[layer, :, :RANK]
            scaling = zs[layer, :, RANK:][:, :1]
            dlatent = (dactive * gelu_slope(latent)).astype(BF)
            dlatent_rows[layer] = dlatent
            inner = jnp.sum(dlatent.astype(F32) * latent, axis=-1, keepdims=True) * (1.0 / WIDTH)
            start, _ = scatter(
                layer, cotangent.at[layer], dlatent_rows.at[layer], kept, sent, sem.at[layer]
            )
            start()

            def passed_on(store):
                for block in range(BLOCKS):
                    unit_grad = lax.dot_general(
                        dlatent, down[layer, block], contract_last, preferred_element_type=F32
                    )
                    unit_rows = hidden[layer, :, span(block)].astype(F32) * scaling
                    passed = cotangent[layer, :, span(block)].astype(F32) + scaling * (
                        unit_grad - unit_rows * inner
                    )
                    store(span(block), passed.astype(BF))

            def store_next(columns, value):
                cotangent[layer - 1, :, columns] = value

            def store_last(columns, value):
                c_out[:, columns] = value

            @pl.when(layer > 0)
            def _():
                passed_on(store_next)

            @pl.when(layer == 0)
            def _():
                passed_on(store_last)

            return carry

        lax.fori_loop(0, LAYERS, one_layer, 0)

        def one_wait(layer, carry):
            _, wait = scatter(
                layer, cotangent.at[layer], dlatent_rows.at[layer], kept, sent, sem.at[layer]
            )
            wait()
            return carry

        lax.fori_loop(0, LAYERS, one_wait, 0)


row_shape = jax.ShapeDtypeStruct((ROWS, WIDTH), BF)
side_shape = pltpu.HBM((2, 2, ROWS, PACKED), BF)
cost = pl.CostEstimate(flops=2 * 10**9, bytes_accessed=40 * 2**20, transcendentals=10**5)


saved_shapes = (
    pltpu.VMEM((LAYERS, ROWS, WIDTH), BF),
    pltpu.VMEM((LAYERS, ROWS, RANK + 128), F32),
    side_shape,
    side_shape,
)


def row_scratch():
    return [
        pltpu.VMEM((LAYERS, ROWS, WIDTH), BF),
        pltpu.VMEM((LAYERS, ROWS, RANK), BF),
        pltpu.SemaphoreType.DMA((LAYERS, 4)),
    ]


def run_first(h_in, entries):
    plan = tuple(what for what, *_ in entries)
    operands = [h_in] + [array for _, *pair in entries for array in pair]
    down, up, h_out, *saved = pl.pallas_call(
        functools.partial(first_kernel, plan),
        out_shape=(
            pltpu.VMEM(down_shape, BF),
            pltpu.VMEM(up_shape, BF),
            row_shape,
            *saved_shapes,
        ),
        in_specs=in_vmem(1) + any_specs(len(operands) - 1),
        out_specs=tuple(in_vmem(5) + any_specs(2)),
        scratch_shapes=[
            *row_scratch(),
            pltpu.SemaphoreType.DMA((LAYERS,)),
            pltpu.SemaphoreType.DMA((LAYERS,)),
        ],
        compiler_params=pltpu.CompilerParams(vmem_limit_bytes=FIRST_LIMIT),
        cost_estimate=cost,
    )(*operands)
    return (down, up), h_out, saved


def run_forward(stage, h_in, weights, saved):
    return pl.pallas_call(
        functools.partial(forward_kernel, stage),
        out_shape=(row_shape, *saved_shapes),
        in_specs=in_vmem(5) + any_specs(2),
        out_specs=tuple(in_vmem(3) + any_specs(2)),
        scratch_shapes=row_scratch(),
        input_output_aliases={3 + i: 1 + i for i in range(4)},
        compiler_params=pltpu.CompilerParams(vmem_limit_bytes=VMEM_LIMIT),
        cost_estimate=cost,
    )(h_in, *weights, *saved)


def run_backward(stage, c_in, hidden, zs, weights, saved, passed=()):
    operands = [c_in, hidden, zs, *weights, *(saved or ()), *passed]
    first = 5 + len(saved or ())
    aliases = {5: 1, 6: 2} if saved else {}
    aliases.update({first + i: 3 + i for i in range(len(passed))})
    return pl.pallas_call(
        functools.partial(backward_kernel, stage, saved is not None, len(passed)),
        out_shape=(
            row_shape,
            side_shape,
            side_shape,
            *[jax.ShapeDtypeStruct(p.shape, p.dtype) for p in passed],
        ),
        in_specs=in_vmem(5) + any_specs(first - 5 + len(passed)),
        out_specs=tuple(in_vmem(1) + any_specs(2 + len(passed))),
        scratch_shapes=[
            pltpu.VMEM((LAYERS, ROWS, WIDTH), BF),
            pltpu.VMEM((LAYERS, ROWS, RANK), BF),
            pltpu.SemaphoreType.DMA((LAYERS, 4)),
        ],
        input_output_aliases=aliases,
        compiler_params=pltpu.CompilerParams(vmem_limit_bytes=VMEM_LIMIT),
        cost_estimate=cost,
    )(*operands)


def ring(block):
    held = {0: block}
    for step in range(1, 5):
        held[step] = along_z(held[step - 1], 1)
        if step < 4:
            held[-step] = along_z(held[1 - step], -1)
    return held


def gather_weights(down_shard, up_shard, needed):
    minor = up_shard[MAJOR:]
    packed = jnp.concatenate([down_shard, minor[:, :RANK], minor[:, RANK:]], axis=0)
    major = ring(exchange_pair(up_shard[:MAJOR]))
    small = ring(packed)
    entries = []
    for members in ((0,), (1, -1), (2, -2), (3, -3), (4,)):
        block = jnp.stack([small[k] for k in members])
        if members[0] == 2:
            block = after(block, *needed)
        full = exchange_pair(block)
        entries.append((("both", members), full, to_core(full)))
    for k in (0, 1, -1, 2, -2, 3, -3, 4):
        entries.append((((0, MAJOR), (k,)), major[k], to_core(major[k])))
    return entries


def exchange(kept, sent):
    other = to_core(sent)
    near = to_first(packed_rows((kept, (1,))))
    far = to_first(packed_rows((other, (1,))))
    early = to_second(packed_rows((kept, (0, 1)), (other, (0, 1))))
    late = to_second(packed_rows((near, (1,)), (far, (1,))))
    return packed_rows(
        (kept, (0, 0)),
        (other, (0, 0)),
        (near, (0,)),
        (far, (0,)),
        (early, ()),
        (late, ()),
    )


def pick(value, index):
    return lax.dynamic_index_in_dim(value, index, 0, keepdims=False)


def body(entering, cotangent, down_proj, up_proj):
    section = lax.axis_index("section")
    y_lo, core = (section // 2) % 2, section % 2

    def own_rows(array, half):
        chosen = pick(array, core).reshape(2, ROWS, 8, 2, BLOCK)
        return pick(chosen, half).swapaxes(1, 2).reshape(ROWS, WIDTH)

    hidden = own_rows(entering, y_lo)
    seeds = own_rows(cotangent, 1 - y_lo)
    entries = gather_weights(down_proj[0], up_proj[0], (hidden, seeds))

    weights, hidden, saved = run_first(hidden, entries)
    incoming = send(
        after(seeds, saved[2]),
        lambda xh, y, c, z, x: (xh, y, c, z, 1 - x),
        lambda xh, y, c, z, x: xh == 1 and y >= 2,
    )
    for stage in range(4):
        if stage > 0:
            hidden, *saved = run_forward(stage, hidden, weights, saved)
        if stage < 3:
            hidden = hop_forward(hidden, stage)
    h_save, zs_save, *sides = saved

    saved = None
    for stage in (3, 2, 1, 0):
        passed = ()
        if stage == 1:
            passed = sides
        if stage == 0:
            passed = (normed,)
        incoming, *saved = run_backward(
            stage, incoming, h_save, zs_save, weights, saved, passed
        )
        saved, passed = saved[:2], saved[2:]
        if stage > 0:
            incoming = hop_backward(incoming, stage)
        if stage == 1:
            normed = exchange(*passed)
    normed = passed[0]
    cotangents = exchange(*saved)

    contract_rows = (((0,), (0,)), ((), ()))

    def partial(wide, narrow):
        return lax.dot_general(
            wide[:, :HALF], narrow[:, HALF:], contract_rows, preferred_element_type=F32
        )

    pieces = jnp.concatenate([partial(normed, cotangents), partial(cotangents, normed)], axis=1)
    groups = [[x + 2 * z for z in range(8)] for x in range(2)]
    totals = lax.psum_scatter(
        pieces.astype(BF), "dp", scatter_dimension=0, axis_index_groups=groups, tiled=True
    ).astype(F32)
    return (totals[:, :RANK][None], totals[:, RANK:].T[None])


def solution(mesh):
    return jax.shard_map(
        body,
        mesh=mesh,
        in_specs=(
            P(None, None, "dp", None),
            P(None, None, "dp", None),
            P("section", "dp", None),
            P("section", None, "dp"),
        ),
        out_specs=(P("section", "dp", None), P("section", None, "dp")),
        check_vma=False,
    )
```
